32 devices in a mesh: pair: 4 (over x, core), virt: 4 (over z), ksplit: 2 (over y).
Axes of the slice: x: 2, y: 2, z: 4, core: 2. Of those that a mesh axis runs over, the one named last changes fastest.
Arguments:
- weights: bfloat16 [1024, 1024], P('virt', 'ksplit'), may hold values from -0.1875 to 0.1875
- amplitudes: bfloat16 [32, 2, 4, 128, 128], P(('pair', 'virt'), 'ksplit'), may hold values from -6 to 6
- slot_tiles: int32 [32, 2, 4], P(('pair', 'virt'), 'ksplit'), may hold values from 0 to 7, as said below
- slot_counts: int32 [32, 2], P(('pair', 'virt'), 'ksplit'), may hold values from 1 to 4
- driving: bfloat16 [32, 1024, 128], P(('pair', 'ksplit'), 'virt'), may hold values from -6 to 6
- virt_energy: float32 [1024], replicated, may hold values from 0.5 to 3
- pair_energy: float32 [32], P(('pair', 'ksplit')), may hold values from -3 to -1
- pair_tile: int32 [32], P(('pair', 'ksplit')), may hold values from 0 to 7
Outputs:
- regrouped: bfloat16 [32, 128, 1024], P(('pair', 'ksplit'), 'virt')
The draws below stay inside these ranges and needn't reach their ends.
Inputs may be any that keep to these rules, and one draw needn't show every extreme that they name: slot_tiles[p, k, s] lies in block k: from k * 4 to (k + 1) * 4 - 1.
All inputs are finite; a program needn't handle non-finite values.
Results may differ from the reference program's by a relative error of at most 0.0065.
Values may be sent and summed in bfloat16 or wider, within the bound.
A program may use at most 128 MiB of HBM per device.

```python
import jax
import jax.numpy as jnp
from jax import lax

TB = 128
NZ_K = 4
NVT = 8
V = 1024
PAIRS = 32
N_KSPLIT = 2


def draw_slot_tiles(key, part):
    key = jax.random.fold_in(key, 11)
    width_block = NVT // N_KSPLIT
    offsets = jax.random.randint(key, (PAIRS, N_KSPLIT, NZ_K), 0, width_block)
    offsets = offsets.at[0, 0, 0].set(0)
    offsets = offsets.at[0, N_KSPLIT - 1, 0].set(width_block - 1)
    starts = jnp.arange(N_KSPLIT, dtype=jnp.int32) * width_block
    return (starts[None, :, None] + offsets).astype(jnp.int32)


def draw_slot_counts(key, part):
    key = jax.random.fold_in(key, 23)
    counts = jax.random.randint(key, (PAIRS, N_KSPLIT), 1, NZ_K + 1)
    counts = counts.at[0, 0].set(NZ_K)
    counts = counts.at[1, 0].set(1)
    return counts.astype(jnp.int32)


def with_ends(values, rng, least, high):
    place = [jax.random.randint(jax.random.fold_in(rng, axis), (), 0, length) for axis, length in enumerate(values.shape)]
    widest = values.shape.index(max(values.shape))
    beside = place[:widest] + [(place[widest] + 1) % values.shape[widest]] + place[widest + 1:]
    return values.at[tuple(place)].set(least).at[tuple(beside)].set(high)


def shard_levels(stream_key, shape, shards, smallest, top_value):
    def one(dim, shards_of):
        steps = jax.random.uniform(jax.random.fold_in(jax.random.fold_in(stream_key, 6), dim), (shards_of,), jnp.float32, smallest / len(shards), top_value / len(shards))
        return jnp.repeat(jnp.exp(steps), shape[dim] // shards_of).reshape((-1,) + (1,) * (len(shape) - dim - 1))

    gain = one(*shards[0])
    for cut in shards[1:]:
        gain = gain * one(*cut)
    return gain


def centred(own_key, shape, deviation, bound, shards=(), kind=jnp.bfloat16):
    factor_of = shard_levels(own_key, shape, shards, -0.22, 0.18) if shards else 1.0
    result = jax.random.normal(own_key, shape, jnp.float32) * deviation * factor_of
    return jnp.minimum(jnp.maximum(result, -bound), bound).astype(kind)


def setup_inputs(seed: int = 0) -> dict:
    splits = jax.random.split(jax.random.key(seed), 9)
    weights = centred(splits[0], (V, V), (NZ_K * N_KSPLIT * TB) ** -0.5, 0.1875, ((0, 4), (1, 2)))
    amplitudes = centred(splits[1], (PAIRS, N_KSPLIT, NZ_K, TB, TB), 1.0, 6.0, ((0, 16), (1, 2)))
    slot_tiles = draw_slot_tiles(jax.random.fold_in(splits[8], 71), 0)
    slot_counts = draw_slot_counts(jax.random.fold_in(splits[8], 71), 0)
    driving = centred(splits[4], (PAIRS, V, TB), 1.0, 6.0, ((0, 8), (1, 4)))
    virt_energy = jnp.clip(jax.random.uniform(splits[5], (V,), jnp.float32, 0.5, 3.0), 0.5, 3.0)
    pair_energy = jnp.clip(-3.0 + 2.0 * jax.random.uniform(splits[6], (PAIRS,), jnp.float32) ** shard_levels(splits[6], (PAIRS,), ((0, 8),), -0.2, 0.2), -3.0, -1.0)
    pair_tile = with_ends(jax.random.randint(splits[7], (PAIRS,), 0, NVT), jax.random.fold_in(splits[7], 1), 0, NVT - 1).astype(jnp.int32)
    return dict(weights=weights, amplitudes=amplitudes, slot_tiles=slot_tiles, slot_counts=slot_counts, driving=driving, virt_energy=virt_energy, pair_energy=pair_energy, pair_tile=pair_tile)


def reference(weights, amplitudes, slot_tiles, slot_counts, driving, virt_energy, pair_energy, pair_tile):
    column_tiles = weights.reshape(V, NVT, TB)
    energy_table = virt_energy.reshape(NVT, TB)

    def one_pair(inputs):
        amps, tiles, counts, drive, energy_pair, tile_pair = inputs
        running = jnp.zeros((V, TB), jnp.float32)
        for split in range(N_KSPLIT):
            chosen = jnp.take(column_tiles, tiles[split], axis=1).astype(jnp.float32)
            live_slot = jnp.arange(NZ_K, dtype=jnp.int32) < counts[split]
            masked = jnp.where(live_slot[:, None, None], amps[split].astype(jnp.float32), jnp.float32(0.0))
            addend = jnp.einsum('asc,scb->ab', chosen, masked).astype(jnp.bfloat16)
            addend = lax.optimization_barrier(addend)
            running = running + addend.astype(jnp.float32)
        cols_energy = jnp.take(energy_table, tile_pair, axis=0)
        denominator = virt_energy[:, None] + cols_energy[None, :] - energy_pair
        updated = ((drive.astype(jnp.float32) + running) / denominator).astype(jnp.bfloat16)
        return updated.T

    return lax.map(one_pair, (amplitudes, slot_tiles, slot_counts, driving, pair_energy, pair_tile))
```

```python
import functools

import jax
import jax.numpy as jnp
from jax import lax
from jax.experimental import pallas as pl
from jax.experimental.pallas import tpu as pltpu
from jax.sharding import PartitionSpec as P

MESH = pl.DeviceIdType.MESH


def gather_body(
    weights, amplitudes, slot_tiles, slot_counts, driving, virt_energy, pair_energy, pair_tile
):
    tile_width = amplitudes.shape[-1]
    slot_number = amplitudes.shape[2]
    rows_local = weights.shape[0]
    blocks_local = weights.shape[1] // tile_width
    split_index = lax.axis_index("ksplit")
    virt_index = lax.axis_index("virt")
    column_tiles = weights.reshape(rows_local, blocks_local, tile_width)
    amps = lax.all_gather(amplitudes, "virt", axis=0, tiled=True)
    tiles = lax.all_gather(slot_tiles, "virt", axis=0, tiled=True)
    counts = lax.all_gather(slot_counts, "virt", axis=0, tiled=True)
    local_ids = tiles[:, 0, :] - split_index * blocks_local
    chosen = jnp.take(column_tiles, local_ids, axis=1)
    live_slot = jnp.arange(slot_number, dtype=jnp.int32)[None, :] < counts
    masked = jnp.where(live_slot[:, :, None, None], amps[:, 0], jnp.zeros((), jnp.bfloat16))
    partial_value = jnp.einsum("apsc,pscb->pab", chosen, masked, preferred_element_type=jnp.float32)
    tile_count = virt_energy.shape[0] // tile_width
    energy_table = virt_energy.reshape(tile_count, tile_width)
    one_hot = (pair_tile[:, None] == jnp.arange(tile_count, dtype=jnp.int32)[None, :]).astype(
        jnp.float32
    )
    cols_energy = jnp.dot(
        one_hot, energy_table, precision=lax.Precision.HIGHEST, preferred_element_type=jnp.float32
    )
    ladder = lax.psum_scatter(
        partial_value.astype(jnp.bfloat16), "ksplit", scatter_dimension=0, tiled=True
    ).astype(jnp.float32)
    rows_energy = lax.dynamic_slice_in_dim(virt_energy, virt_index * rows_local, rows_local)
    denominator = rows_energy[None, :, None] + cols_energy[:, None, :] - pair_energy[:, None, None]
    updated = ((driving.astype(jnp.float32) + ladder) / denominator).astype(jnp.bfloat16)
    flipped = jnp.swapaxes(updated, 1, 2)
    return lax.all_to_all(flipped, "virt", split_axis=1, concat_axis=2, tiled=True)


NQ, NV, NK = 4, 4, 2


def kernel(
    tiles_ref,
    counts_ref,
    pair_tile_ref,
    pair_energy_ref,
    w_hbm,
    amps_hbm,
    driving_hbm,
    energy_ref,
    out_ref,
    w_all,
    amps_in,
    driving_in,
    amps_tx,
    amps_rx,
    driving_tx,
    driving_rx,
    local_sem,
    z_send,
    z_recv,
    y_send,
    y_recv,
    x_send,
    x_recv,
    c_send,
    c_recv,
    a_send,
    a_recv,
    d_send,
    d_recv,
):
    q = lax.axis_index("pair")
    v = lax.axis_index("virt")
    y = lax.axis_index("ksplit")
    other_y = 1 - y
    core_q = q + 1 - 2 * lax.rem(q, 2)
    far_q = lax.rem(q + 2, NQ)
    far_core_q = lax.rem(core_q + 2, NQ)
    pairs_in, slots, tile, _ = amps_in.shape
    pairs_out = driving_in.shape[0]
    chunk = tile // NV
    block_tiles = amps_tx.shape[-1] // tile
    rows_local = driving_in.shape[1]

    w_load = pltpu.make_async_copy(w_hbm, w_all.at[y, v], local_sem.at[0])
    amps_load = pltpu.make_async_copy(amps_hbm, amps_in, local_sem.at[1])
    driving_load = pltpu.make_async_copy(driving_hbm, driving_in, local_sem.at[2])
    w_load.start()
    amps_load.start()
    driving_load.start()

    barrier = pltpu.get_barrier_semaphore()
    peers = [(q, lax.rem(v + r, NV), y) for r in range(1, NV)]
    peers += [(q, lax.rem(v + r, NV), other_y) for r in range(NV)]
    peers += [(core_q, v, y), (far_q, v, y)]
    for peer in peers:
        pl.semaphore_signal(barrier, inc=1, device_id=peer, device_id_type=MESH)
    pl.semaphore_wait(barrier, len(peers))

    sent = []

    def send(src, dst, send_sem, recv_sem, device):
        copy = pltpu.make_async_remote_copy(
            src_ref=src, dst_ref=dst, send_sem=send_sem, recv_sem=recv_sem,
            device_id=device, device_id_type=MESH,
        )
        copy.start()
        sent.append(copy)

    def arrived(dst, sem):
        pltpu.make_async_remote_copy(
            src_ref=dst, dst_ref=dst, send_sem=sem, recv_sem=sem,
            device_id=(core_q, v, y), device_id_type=MESH,
        ).wait_recv()

    def piece(split, virt, quarter):
        return w_all.at[split, virt, quarter]

    w_load.wait()
    own = piece(y, v, q)
    for r in (2, 1, 3):
        send(own, own, z_send.at[r], z_recv.at[r], (q, lax.rem(v + r, NV), y))
    send(own, own, y_send.at[0], y_recv.at[0], (q, v, other_y))

    amps_load.wait()
    for i in range(pairs_in):
        count = counts_ref[i, 0]
        loaded = [amps_in[i, s].astype(jnp.float32) for s in range(slots)]
        for t in range(block_tiles):
            total = jnp.zeros((tile, tile), jnp.float32)
            for s in range(slots):
                use = jnp.logical_and(count > s, tiles_ref[i, s] == y * block_tiles + t)
                total = total + jnp.where(use, 1.0, 0.0).astype(jnp.float32) * loaded[s]
            flipped = total.T.astype(jnp.bfloat16)
            for j in range(NV):
                amps_tx[j, i, :, t * tile:(t + 1) * tile] = flipped[j * chunk:(j + 1) * chunk]
    owner_y = v // 2
    half = lax.rem(v, 2)
    a_slot = half * NK + y
    a_dst = amps_rx.at[y, half]
    for r in (2, 1, 3):
        to = lax.rem(v + r, NV)
        send(amps_tx.at[to], a_dst, a_send.at[r], a_recv.at[a_slot], (q, to, owner_y))

    @pl.when(owner_y == y)
    def _():
        copy = pltpu.make_async_copy(amps_tx.at[v], a_dst, local_sem.at[1])
        copy.start()
        copy.wait()

    @pl.when(owner_y != y)
    def _():
        pltpu.make_async_remote_copy(
            src_ref=amps_tx.at[v], dst_ref=a_dst, send_sem=a_send.at[0], recv_sem=a_recv.at[a_slot],
            device_id=(q, v, other_y), device_id_type=MESH,
        ).start()

    driving_load.wait()
    for i in range(pairs_out):
        for h in range(rows_local // tile):
            flipped = driving_in[i, h * tile:(h + 1) * tile].astype(jnp.float32).T.astype(jnp.bfloat16)
            for j in range(NV):
                driving_tx[j, i, :, h * tile:(h + 1) * tile] = flipped[j * chunk:(j + 1) * chunk]
    for r in (2, 1, 3):
        to = lax.rem(v + r, NV)
        send(driving_tx.at[to], driving_rx.at[v], d_send.at[r], d_recv.at[r], (q, to, y))
    driving_own = pltpu.make_async_copy(driving_tx.at[v], driving_rx.at[v], local_sem.at[2])
    driving_own.start()

    order = (0, 1, 3, 2)
    for r in order:
        s = lax.rem(v + NV - r, NV)
        if r:
            got = piece(y, s, q)
            arrived(got, z_recv.at[r])
            send(got, got, y_send.at[r], y_recv.at[r], (q, v, other_y))
            send(got, got, x_send.at[r, 0], x_recv.at[r, 0], (far_q, v, y))
            send(got, got, c_send.at[r, 0, 0], c_recv.at[r, 0, 0], (core_q, v, y))
    for r in order:
        s = lax.rem(v + NV - r, NV)
        got = piece(other_y, s, q)
        arrived(got, y_recv.at[r])
        send(got, got, x_send.at[r, 1], x_recv.at[r, 1], (far_q, v, y))
        send(got, got, c_send.at[r, 1, 0], c_recv.at[r, 1, 0], (core_q, v, y))
    for r in order:
        s = lax.rem(v + NV - r, NV)
        for n, split in ((0, y), (1, other_y)):
            if r or n:
                got = piece(split, s, far_q)
                arrived(got, x_recv.at[r, n])
                send(got, got, c_send.at[r, n, 1], c_recv.at[r, n, 1], (core_q, v, y))
    for r in order:
        s = lax.rem(v + NV - r, NV)
        for n, split in ((0, y), (1, other_y)):
            if r or n:
                arrived(piece(split, s, core_q), c_recv.at[r, n, 0])
                arrived(piece(split, s, far_core_q), c_recv.at[r, n, 1])

    for src_half in range(2):
        for src_y in range(NK):
            slot = src_half * NK + src_y
            mine = jnp.logical_and(v == y * 2 + src_half, y == src_y)

            @pl.when(jnp.logical_not(mine))
            def _():
                arrived(amps_rx.at[src_y, src_half], a_recv.at[slot])

    driving_own.wait()
    for r in (1, 3, 2):
        s = lax.rem(v + NV - r, NV)
        arrived(driving_rx.at[s], d_recv.at[r])

    rows = pairs_out * chunk
    lane = lax.broadcasted_iota(jnp.int32, (chunk, tile), 1)
    row = lax.broadcasted_iota(jnp.int32, (chunk, tile), 0)
    picked = lane == row + v * chunk
    shifts = []
    for i in range(pairs_out):
        line = energy_ref[pair_tile_ref[i]]
        column = jnp.sum(jnp.where(picked, line, 0.0), axis=1, keepdims=True)
        shifts.append((column, pair_energy_ref[i]))
    left = [amps_rx[k].reshape(rows, amps_rx.shape[-1]) for k in range(NK)]
    per_tile = rows_local // tile
    for s in range(NV):
        ladder = jnp.zeros((rows, rows_local), jnp.float32)
        for k in range(NK):
            block = w_all[k, s].reshape(rows_local, w_all.shape[-1])
            ladder = ladder + lax.dot_general(
                left[k], block, (((1,), (1,)), ((), ())), preferred_element_type=jnp.float32
            )
        for i in range(pairs_out):
            column, pair = shifts[i]
            for h in range(per_tile):
                lanes = slice(h * tile, (h + 1) * tile)
                denominator = energy_ref[s * per_tile + h] + column - pair
                value = driving_rx[s, i, :, lanes].astype(jnp.float32)
                value = value + ladder[i * chunk:(i + 1) * chunk, lanes]
                out_ref[i, :, s * rows_local + h * tile:s * rows_local + (h + 1) * tile] = (
                    value / denominator
                ).astype(jnp.bfloat16)

    for copy in sent:
        copy.wait_send()

    @pl.when(owner_y != y)
    def _():
        pltpu.make_async_remote_copy(
            src_ref=amps_tx.at[v], dst_ref=a_dst, send_sem=a_send.at[0], recv_sem=a_recv.at[a_slot],
            device_id=(q, v, other_y), device_id_type=MESH,
        ).wait_send()


def fused_body(
    weights, amplitudes, slot_tiles, slot_counts, driving, virt_energy, pair_energy, pair_tile
):
    pairs_in, _, slots, tile, _ = amplitudes.shape
    rows_local, columns = weights.shape
    pairs_out = driving.shape[0]
    chunk = tile // NV
    whole_rows = virt_energy.shape[0]
    bf16 = jnp.bfloat16
    dma = pltpu.SemaphoreType.DMA
    smem = pl.BlockSpec(memory_space=pltpu.SMEM)
    hbm = pl.BlockSpec(memory_space=pl.ANY)
    vmem = pl.BlockSpec(memory_space=pltpu.VMEM)
    return pl.pallas_call(
        kernel,
        out_shape=jax.ShapeDtypeStruct((pairs_out, chunk, whole_rows), bf16),
        in_specs=[smem, smem, smem, smem, hbm, hbm, hbm, vmem],
        out_specs=vmem,
        scratch_shapes=[
            pltpu.VMEM((NK, NV, NQ, rows_local // NQ, columns), bf16),
            pltpu.VMEM((pairs_in, slots, tile, tile), bf16),
            pltpu.VMEM((pairs_out, rows_local, tile), bf16),
            pltpu.VMEM((NV, pairs_in, chunk, columns), bf16),
            pltpu.VMEM((NK, 2, pairs_in, chunk, columns), bf16),
            pltpu.VMEM((NV, pairs_out, chunk, rows_local), bf16),
            pltpu.VMEM((NV, pairs_out, chunk, rows_local), bf16),
            dma((3,)),
            dma((NV,)),
            dma((NV,)),
            dma((NV,)),
            dma((NV,)),
            dma((NV, 2)),
            dma((NV, 2)),
            dma((NV, 2, 2)),
            dma((NV, 2, 2)),
            dma((NV,)),
            dma((2 * NK,)),
            dma((NV,)),
            dma((NV,)),
        ],
        compiler_params=pltpu.CompilerParams(
            collective_id=0, has_side_effects=True, vmem_limit_bytes=24 * 1024 * 1024
        ),
        cost_estimate=pl.CostEstimate(
            flops=2 * pairs_out * chunk * whole_rows * columns * NK,
            bytes_accessed=4 * 2 * rows_local * columns,
            transcendentals=0,
        ),
    )(
        slot_tiles.reshape(pairs_in, slots),
        slot_counts,
        pair_tile,
        pair_energy,
        weights.reshape(NQ, rows_local // NQ, columns),
        amplitudes.reshape(pairs_in, slots, tile, tile),
        driving,
        virt_energy.reshape(whole_rows // tile, 1, tile),
    )


def solution(mesh):
    placed = (
        P("virt", "ksplit"),
        P(("pair", "virt"), "ksplit", None, None, None),
        P(("pair", "virt"), "ksplit", None),
        P(("pair", "virt"), "ksplit"),
        P(("pair", "ksplit"), "virt", None),
        P(),
        P(("pair", "ksplit")),
        P(("pair", "ksplit")),
    )
    sizes = dict(mesh.shape)
    plan = (sizes["pair"], sizes["virt"], sizes["ksplit"]) == (NQ, NV, NK)

    def chosen(weights, amplitudes, *rest):
        slots, tile = amplitudes.shape[2], amplitudes.shape[3]
        small = weights.size <= 2 ** 21 and weights.shape[1] == 2 * NK * 2 * tile
        pairs = amplitudes.shape[0] == 2 * NQ * NV
        return jax.shard_map(
            fused_body if plan and small and pairs else gather_body,
            mesh=mesh,
            in_specs=placed,
            out_specs=P(("pair", "ksplit"), "virt", None),
            check_vma=False,
        )(weights, amplitudes, *rest)

    return chosen
```

```python
import jax
import jax.numpy as jnp
from jax import lax
from jax.experimental import pallas as pl
from jax.experimental.pallas import tpu as pltpu
from jax.sharding import PartitionSpec as P

MESH = pl.DeviceIdType.MESH


def gather_body(
    weights, amplitudes, slot_tiles, slot_counts, driving, virt_energy, pair_energy, pair_tile
):
    tile_width = amplitudes.shape[-1]
    slot_number = amplitudes.shape[2]
    rows_local = weights.shape[0]
    blocks_local = weights.shape[1] // tile_width
    split_index = lax.axis_index("ksplit")
    virt_index = lax.axis_index("virt")
    column_tiles = weights.reshape(rows_local, blocks_local, tile_width)
    amps = lax.all_gather(amplitudes, "virt", axis=0, tiled=True)
    tiles = lax.all_gather(slot_tiles, "virt", axis=0, tiled=True)
    counts = lax.all_gather(slot_counts, "virt", axis=0, tiled=True)
    local_ids = tiles[:, 0, :] - split_index * blocks_local
    chosen = jnp.take(column_tiles, local_ids, axis=1)
    live_slot = jnp.arange(slot_number, dtype=jnp.int32)[None, :] < counts
    masked = jnp.where(live_slot[:, :, None, None], amps[:, 0], jnp.zeros((), jnp.bfloat16))
    partial_value = jnp.einsum("apsc,pscb->pab", chosen, masked, preferred_element_type=jnp.float32)
    tile_count = virt_energy.shape[0] // tile_width
    energy_table = virt_energy.reshape(tile_count, tile_width)
    one_hot = (pair_tile[:, None] == jnp.arange(tile_count, dtype=jnp.int32)[None, :]).astype(
        jnp.float32
    )
    cols_energy = jnp.dot(
        one_hot, energy_table, precision=lax.Precision.HIGHEST, preferred_element_type=jnp.float32
    )
    ladder = lax.psum_scatter(
        partial_value.astype(jnp.bfloat16), "ksplit", scatter_dimension=0, tiled=True
    ).astype(jnp.float32)
    rows_energy = lax.dynamic_slice_in_dim(virt_energy, virt_index * rows_local, rows_local)
    denominator = rows_energy[None, :, None] + cols_energy[:, None, :] - pair_energy[:, None, None]
    updated = ((driving.astype(jnp.float32) + ladder) / denominator).astype(jnp.bfloat16)
    flipped = jnp.swapaxes(updated, 1, 2)
    return lax.all_to_all(flipped, "virt", split_axis=1, concat_axis=2, tiled=True)


NQ, NV, NK = 4, 4, 2


def kernel(
    tiles_hbm,
    counts_hbm,
    pair_tile_hbm,
    pair_energy_hbm,
    w_hbm,
    amps_hbm,
    driving_hbm,
    energy_hbm,
    out_ref,
    tiles_ref,
    counts_ref,
    pair_tile_ref,
    pair_energy_ref,
    energy_ref,
    w_all,
    amps_in,
    driving_in,
    amps_tx,
    amps_rx,
    driving_tx,
    driving_rx,
    ladder_ref,
    local_sem,
    z_send,
    z_recv,
    y_send,
    y_recv,
    x_send,
    x_recv,
    c_send,
    c_recv,
    a_send,
    a_recv,
    d_send,
    d_recv,
):
    q = lax.axis_index("pair")
    v = lax.axis_index("virt")
    y = lax.axis_index("ksplit")
    other_y = 1 - y
    core_q = q + 1 - 2 * lax.rem(q, 2)
    far_q = lax.rem(q + 2, NQ)
    far_core_q = lax.rem(core_q + 2, NQ)
    first = v + 1 - 2 * lax.rem(v, 2)
    second = 2 - v // 2
    third = 3 - 3 * (v // 2)
    inner = jnp.logical_or(v == 1, v == 2)
    pairs_in, slots, tile, _ = amps_in.shape
    pairs_out = driving_in.shape[0]
    chunk = tile // NV
    block_tiles = amps_tx.shape[-1] // tile
    rows_local = driving_in.shape[1]

    loads = [
        pltpu.make_async_copy(src, dst, local_sem.at[n])
        for n, (src, dst) in enumerate((
            (amps_hbm, amps_in),
            (w_hbm, w_all.at[y, v]),
            (tiles_hbm, tiles_ref),
            (counts_hbm, counts_ref),
            (driving_hbm, driving_in),
            (pair_tile_hbm, pair_tile_ref),
            (pair_energy_hbm, pair_energy_ref),
            (energy_hbm, energy_ref),
        ))
    ]
    for load in loads:
        load.start()
    amps_load, w_load, tiles_load, counts_load, driving_load, *other_loads = loads

    barrier = pltpu.get_barrier_semaphore()
    peers = [(q, lax.rem(v + r, NV), y) for r in range(1, NV)]
    peers += [(q, lax.rem(v + r, NV), other_y) for r in range(NV)]
    peers += [(core_q, v, y), (far_q, v, y)]
    for peer in peers:
        pl.semaphore_signal(barrier, inc=1, device_id=peer, device_id_type=MESH)
    w_load.wait()
    pl.semaphore_wait(barrier, len(peers))

    sent = []

    def send(src, dst, send_sem, recv_sem, device, when=None):
        copy = pltpu.make_async_remote_copy(
            src_ref=src, dst_ref=dst, send_sem=send_sem, recv_sem=recv_sem,
            device_id=device, device_id_type=MESH,
        )
        if when is None:
            copy.start()
        else:
            pl.when(when)(copy.start)
        sent.append((copy, when))

    def arrived(dst, sem):
        pltpu.make_async_remote_copy(
            src_ref=dst, dst_ref=dst, send_sem=sem, recv_sem=sem,
            device_id=(core_q, v, y), device_id_type=MESH,
        ).wait_recv()

    own = w_all.at[y, v, q]
    send(own, own, z_send.at[v, 1], z_recv.at[v], (q, second, y), inner)
    send(own, own, z_send.at[v, 0], z_recv.at[v], (q, first, y))
    send(own, own, y_send.at[v], y_recv.at[v], (q, v, other_y))

    amps_load.wait()
    tiles_load.wait()
    counts_load.wait()
    for i in range(pairs_in):
        count = counts_ref[i]
        loaded = [amps_in[i, s].astype(jnp.float32) for s in range(slots)]
        for t in range(block_tiles):
            total = jnp.zeros((tile, tile), jnp.float32)
            for s in range(slots):
                use = jnp.logical_and(count > s, tiles_ref[i, 0, s] == y * block_tiles + t)
                total = total + jnp.where(use, 1.0, 0.0).astype(jnp.float32) * loaded[s]
            flipped = total.T.astype(jnp.bfloat16)
            for j in range(NV):
                amps_tx[j, i, :, t * tile:(t + 1) * tile] = flipped[j * chunk:(j + 1) * chunk]
    owner_y = v // 2
    half = lax.rem(v, 2)
    a_slot = half * NK + y
    a_dst = amps_rx.at[y, half]
    for to in (third, second, first):
        send(amps_tx.at[to], a_dst, a_send.at[to], a_recv.at[a_slot], (q, to, owner_y))
    own_amps = pltpu.make_async_copy(amps_tx.at[v], a_dst, local_sem.at[0])
    pl.when(owner_y == y)(own_amps.start)
    send(amps_tx.at[v], a_dst, a_send.at[v], a_recv.at[a_slot], (q, v, other_y), owner_y != y)

    driving_load.wait()
    for i in range(pairs_out):
        for h in range(rows_local // tile):
            flipped = driving_in[i, h * tile:(h + 1) * tile].astype(jnp.float32).T.astype(jnp.bfloat16)
            for j in range(NV):
                driving_tx[j, i, :, h * tile:(h + 1) * tile] = flipped[j * chunk:(j + 1) * chunk]
    for to in (third, second, first):
        send(driving_tx.at[to], driving_rx.at[v], d_send.at[to], d_recv.at[v], (q, to, y))
    own_driving = pltpu.make_async_copy(driving_tx.at[v], driving_rx.at[v], local_sem.at[1])
    own_driving.start()

    def from_virt(s, to, when):
        got = w_all.at[y, s, q]
        arrived(got, z_recv.at[s])
        send(got, got, z_send.at[s, 0], z_recv.at[s], (q, to, y), when)
        send(got, got, y_send.at[s], y_recv.at[s], (q, v, other_y))
        send(got, got, x_send.at[s, 0], x_recv.at[s, 0], (far_q, v, y))
        send(got, got, c_send.at[s, 0, 0], c_recv.at[s, 0, 0], (core_q, v, y))

    def from_split(s):
        got = w_all.at[other_y, s, q]
        arrived(got, y_recv.at[s])
        send(got, got, x_send.at[s, 1], x_recv.at[s, 1], (far_q, v, y))
        send(got, got, c_send.at[s, 1, 0], c_recv.at[s, 1, 0], (core_q, v, y))

    def from_far(s, n):
        got = w_all.at[(y, other_y)[n], s, far_q]
        arrived(got, x_recv.at[s, n])
        send(got, got, c_send.at[s, n, 1], c_recv.at[s, n, 1], (core_q, v, y))

    from_virt(first, second, inner)
    from_split(v)
    from_virt(second, first, inner)
    from_split(first)
    from_far(v, 1)
    from_far(first, 0)
    from_virt(third, first, inner)
    from_split(second)
    from_far(first, 1)
    from_far(second, 0)
    from_split(third)
    from_far(second, 1)
    from_far(third, 0)
    from_far(third, 1)

    pl.when(owner_y == y)(own_amps.wait)
    for src_half in range(2):
        for src_y in range(NK):
            mine = jnp.logical_and(v == y * 2 + src_half, y == src_y)

            @pl.when(jnp.logical_not(mine))
            def _():
                arrived(amps_rx.at[src_y, src_half], a_recv.at[src_half * NK + src_y])

    rows = pairs_out * chunk
    left = [amps_rx[k].reshape(rows, amps_rx.shape[-1]) for k in range(NK)]
    for s in (v, first, second, third):
        for n in range(NK):
            if n or s is not v:
                split = (y, other_y)[n]
                arrived(w_all.at[split, s, core_q], c_recv.at[s, n, 0])
                arrived(w_all.at[split, s, far_core_q], c_recv.at[s, n, 1])
        ladder = jnp.zeros((rows, rows_local), jnp.float32)
        for k in range(NK):
            block = w_all[k, s].reshape(rows_local, w_all.shape[-1])
            ladder = ladder + lax.dot_general(
                left[k], block, (((1,), (1,)), ((), ())), preferred_element_type=jnp.float32
            )
        ladder_ref[s] = ladder

    for load in other_loads:
        load.wait()
    lane = lax.broadcasted_iota(jnp.int32, (chunk, tile), 1)
    row = lax.broadcasted_iota(jnp.int32, (chunk, tile), 0)
    picked = lane == row + v * chunk
    shifts = []
    for i in range(pairs_out):
        line = energy_ref[pair_tile_ref[i]]
        column = jnp.sum(jnp.where(picked, line, 0.0), axis=1, keepdims=True)
        shifts.append((column, pair_energy_ref[i]))
    per_tile = rows_local // tile
    own_driving.wait()
    for s in (first, second, third):
        arrived(driving_rx.at[s], d_recv.at[s])
    for s in range(NV):
        for i in range(pairs_out):
            column, pair = shifts[i]
            for h in range(per_tile):
                lanes = slice(h * tile, (h + 1) * tile)
                denominator = energy_ref[s * per_tile + h] + column - pair
                value = driving_rx[s, i, :, lanes].astype(jnp.float32)
                value = value + ladder_ref[s, i * chunk:(i + 1) * chunk, lanes]
                out_ref[i, :, s * rows_local + h * tile:s * rows_local + (h + 1) * tile] = (
                    value / denominator
                ).astype(jnp.bfloat16)

    for copy, when in sent:
        if when is None:
            copy.wait_send()
        else:
            pl.when(when)(copy.wait_send)


def fused_body(
    weights, amplitudes, slot_tiles, slot_counts, driving, virt_energy, pair_energy, pair_tile
):
    pairs_in, _, slots, tile, _ = amplitudes.shape
    rows_local, columns = weights.shape
    pairs_out = driving.shape[0]
    chunk = tile // NV
    whole_rows = virt_energy.shape[0]
    bf16 = jnp.bfloat16
    dma = pltpu.SemaphoreType.DMA
    hbm = pl.BlockSpec(memory_space=pltpu.HBM)
    return pl.pallas_call(
        kernel,
        out_shape=jax.ShapeDtypeStruct((pairs_out, chunk, whole_rows), bf16),
        in_specs=[hbm] * 8,
        out_specs=pl.BlockSpec(memory_space=pltpu.VMEM),
        scratch_shapes=[
            pltpu.SMEM((pairs_in, 1, slots), jnp.int32),
            pltpu.SMEM((pairs_in,), jnp.int32),
            pltpu.SMEM((pairs_out,), jnp.int32),
            pltpu.SMEM((pairs_out,), jnp.float32),
            pltpu.VMEM((whole_rows // tile, 1, tile), jnp.float32),
            pltpu.VMEM((NK, NV, NQ, rows_local // NQ, columns), bf16),
            pltpu.VMEM((pairs_in, slots, tile, tile), bf16),
            pltpu.VMEM((pairs_out, rows_local, tile), bf16),
            pltpu.VMEM((NV, pairs_in, chunk, columns), bf16),
            pltpu.VMEM((NK, 2, pairs_in, chunk, columns), bf16),
            pltpu.VMEM((NV, pairs_out, chunk, rows_local), bf16),
            pltpu.VMEM((NV, pairs_out, chunk, rows_local), bf16),
            pltpu.VMEM((NV, pairs_out * chunk, rows_local), jnp.float32),
            dma((8,)),
            dma((NV, 2)),
            dma((NV,)),
            dma((NV,)),
            dma((NV,)),
            dma((NV, 2)),
            dma((NV, 2)),
            dma((NV, 2, 2)),
            dma((NV, 2, 2)),
            dma((NV,)),
            dma((2 * NK,)),
            dma((NV,)),
            dma((NV,)),
        ],
        compiler_params=pltpu.CompilerParams(
            collective_id=0, has_side_effects=True, vmem_limit_bytes=56 * 1024 * 1024
        ),
        cost_estimate=pl.CostEstimate(
            flops=2 * pairs_out * chunk * whole_rows * columns * NK,
            bytes_accessed=4 * 2 * rows_local * columns,
            transcendentals=0,
        ),
    )(
        slot_tiles,
        slot_counts.reshape(pairs_in),
        pair_tile,
        pair_energy,
        weights.reshape(NQ, rows_local // NQ, columns),
        amplitudes.reshape(pairs_in, slots, tile, tile),
        driving,
        virt_energy.reshape(whole_rows // tile, 1, tile),
    )


def solution(mesh):
    placed = (
        P("virt", "ksplit"),
        P(("pair", "virt"), "ksplit", None, None, None),
        P(("pair", "virt"), "ksplit", None),
        P(("pair", "virt"), "ksplit"),
        P(("pair", "ksplit"), "virt", None),
        P(),
        P(("pair", "ksplit")),
        P(("pair", "ksplit")),
    )
    sizes = dict(mesh.shape)
    plan = (sizes["pair"], sizes["virt"], sizes["ksplit"]) == (NQ, NV, NK)

    def chosen(weights, amplitudes, *rest):
        slots, tile = amplitudes.shape[2], amplitudes.shape[3]
        small = weights.size <= 2 ** 21 and weights.shape[1] == 2 * NK * 2 * tile
        pairs = amplitudes.shape[0] == 2 * NQ * NV
        return jax.shard_map(
            fused_body if plan and small and pairs else gather_body,
            mesh=mesh,
            in_specs=placed,
            out_specs=P(("pair", "ksplit"), "virt", None),
            check_vma=False,
        )(weights, amplitudes, *rest)

    return chosen
```

```python
import jax
import jax.numpy as jnp
from jax import lax
from jax.experimental import pallas as pl
from jax.experimental.pallas import tpu as pltpu
from jax.sharding import PartitionSpec as P

MESH = pl.DeviceIdType.MESH


def gather_body(
    weights, amplitudes, slot_tiles, slot_counts, driving, virt_energy, pair_energy, pair_tile
):
    tile_width = amplitudes.shape[-1]
    slot_number = amplitudes.shape[2]
    rows_local = weights.shape[0]
    blocks_local = weights.shape[1] // tile_width
    split_index = lax.axis_index("ksplit")
    virt_index = lax.axis_index("virt")
    column_tiles = weights.reshape(rows_local, blocks_local, tile_width)
    amps = lax.all_gather(amplitudes, "virt", axis=0, tiled=True)
    tiles = lax.all_gather(slot_tiles, "virt", axis=0, tiled=True)
    counts = lax.all_gather(slot_counts, "virt", axis=0, tiled=True)
    local_ids = tiles[:, 0, :] - split_index * blocks_local
    chosen = jnp.take(column_tiles, local_ids, axis=1)
    live_slot = jnp.arange(slot_number, dtype=jnp.int32)[None, :] < counts
    masked = jnp.where(live_slot[:, :, None, None], amps[:, 0], jnp.zeros((), jnp.bfloat16))
    partial_value = jnp.einsum("apsc,pscb->pab", chosen, masked, preferred_element_type=jnp.float32)
    tile_count = virt_energy.shape[0] // tile_width
    energy_table = virt_energy.reshape(tile_count, tile_width)
    one_hot = (pair_tile[:, None] == jnp.arange(tile_count, dtype=jnp.int32)[None, :]).astype(
        jnp.float32
    )
    cols_energy = jnp.dot(
        one_hot, energy_table, precision=lax.Precision.HIGHEST, preferred_element_type=jnp.float32
    )
    ladder = lax.psum_scatter(
        partial_value.astype(jnp.bfloat16), "ksplit", scatter_dimension=0, tiled=True
    ).astype(jnp.float32)
    rows_energy = lax.dynamic_slice_in_dim(virt_energy, virt_index * rows_local, rows_local)
    denominator = rows_energy[None, :, None] + cols_energy[:, None, :] - pair_energy[:, None, None]
    updated = ((driving.astype(jnp.float32) + ladder) / denominator).astype(jnp.bfloat16)
    flipped = jnp.swapaxes(updated, 1, 2)
    return lax.all_to_all(flipped, "virt", split_axis=1, concat_axis=2, tiled=True)


NQ, NV, NK = 4, 4, 2


def kernel(
    tiles_hbm,
    counts_hbm,
    pair_tile_hbm,
    pair_energy_hbm,
    w_hbm,
    amps_hbm,
    driving_hbm,
    energy_hbm,
    out_ref,
    tiles_ref,
    counts_ref,
    pair_tile_ref,
    pair_energy_ref,
    energy_ref,
    w_all,
    amps_in,
    driving_in,
    amps_tx,
    amps_rx,
    driving_tx,
    driving_rx,
    ladder_ref,
    local_sem,
    z_send,
    z_recv,
    y_send,
    y_recv,
    x_send,
    x_recv,
    c_send,
    c_recv,
    a_send,
    a_recv,
    d_send,
    d_recv,
):
    q = lax.axis_index("pair")
    v = lax.axis_index("virt")
    y = lax.axis_index("ksplit")
    other_y = 1 - y
    core_q = q + 1 - 2 * lax.rem(q, 2)
    far_q = lax.rem(q + 2, NQ)
    far_core_q = lax.rem(core_q + 2, NQ)
    first = v + 1 - 2 * lax.rem(v, 2)
    second = 2 - v // 2
    third = 3 - 3 * (v // 2)
    pairs_in, slots, tile, _ = amps_in.shape
    pairs_out = driving_in.shape[0]
    chunk = tile // NV
    block_tiles = amps_tx.shape[-1] // tile
    rows_local = driving_in.shape[1]

    loads = [
        pltpu.make_async_copy(src, dst, local_sem.at[n])
        for n, (src, dst) in enumerate((
            (amps_hbm, amps_in),
            (w_hbm, w_all.at[y, v]),
            (tiles_hbm, tiles_ref),
            (counts_hbm, counts_ref),
            (driving_hbm, driving_in),
            (pair_tile_hbm, pair_tile_ref),
            (pair_energy_hbm, pair_energy_ref),
            (energy_hbm, energy_ref),
        ))
    ]
    for load in loads:
        load.start()
    amps_load, w_load, tiles_load, counts_load, driving_load, *other_loads = loads

    barrier = pltpu.get_barrier_semaphore()
    peers = [(q, lax.rem(v + r, NV), y) for r in range(1, NV)]
    peers += [(q, lax.rem(v + r, NV), other_y) for r in range(NV)]
    peers += [(core_q, v, y), (far_q, v, y), (far_q, v, other_y)]
    for peer in peers:
        pl.semaphore_signal(barrier, inc=1, device_id=peer, device_id_type=MESH)
    w_load.wait()
    pl.semaphore_wait(barrier, len(peers))

    sent = []

    def send(src, dst, send_sem, recv_sem, device, when=None):
        copy = pltpu.make_async_remote_copy(
            src_ref=src, dst_ref=dst, send_sem=send_sem, recv_sem=recv_sem,
            device_id=device, device_id_type=MESH,
        )
        if when is None:
            copy.start()
        else:
            pl.when(when)(copy.start)
        sent.append((copy, when))

    def arrived(dst, sem):
        pltpu.make_async_remote_copy(
            src_ref=dst, dst_ref=dst, send_sem=sem, recv_sem=sem,
            device_id=(core_q, v, y), device_id_type=MESH,
        ).wait_recv()

    own = w_all.at[y, v, q]
    for to in (first, second, third):
        send(own, own, z_send.at[to], z_recv.at[v], (q, to, y))
    send(own, own, y_send.at[v], y_recv.at[v], (q, v, other_y))
    send(own, own, x_send.at[v, 1], x_recv.at[v, 1], (far_q, v, other_y))

    amps_load.wait()
    tiles_load.wait()
    counts_load.wait()
    for i in range(pairs_in):
        count = counts_ref[i]
        loaded = [amps_in[i, s].astype(jnp.float32) for s in range(slots)]
        for t in range(block_tiles):
            total = jnp.zeros((tile, tile), jnp.float32)
            for s in range(slots):
                use = jnp.logical_and(count > s, tiles_ref[i, 0, s] == y * block_tiles + t)
                total = total + jnp.where(use, 1.0, 0.0).astype(jnp.float32) * loaded[s]
            flipped = total.T.astype(jnp.bfloat16)
            for j in range(NV):
                amps_tx[j, i, :, t * tile:(t + 1) * tile] = flipped[j * chunk:(j + 1) * chunk]
    owner_y = v // 2
    half = lax.rem(v, 2)
    a_slot = half * NK + y
    a_dst = amps_rx.at[y, half]
    for to in (third, second, first):
        send(amps_tx.at[to], a_dst, a_send.at[to], a_recv.at[a_slot], (q, to, owner_y))
    own_amps = pltpu.make_async_copy(amps_tx.at[v], a_dst, local_sem.at[0])
    pl.when(owner_y == y)(own_amps.start)
    send(amps_tx.at[v], a_dst, a_send.at[v], a_recv.at[a_slot], (q, v, other_y), owner_y != y)

    def from_virt(s):
        got = w_all.at[y, s, q]
        arrived(got, z_recv.at[s])
        send(got, got, x_send.at[s, 0], x_recv.at[s, 0], (far_q, v, y))
        send(got, got, x_send.at[s, 1], x_recv.at[s, 1], (far_q, v, other_y))
        send(got, got, y_send.at[s], y_recv.at[s], (q, v, other_y))
        send(got, got, c_send.at[s, 0, 0], c_recv.at[s, 0, 0], (core_q, v, y))

    def from_split(s):
        got = w_all.at[other_y, s, q]
        arrived(got, y_recv.at[s])
        send(got, got, c_send.at[s, 1, 0], c_recv.at[s, 1, 0], (core_q, v, y))

    def from_far(s, n):
        got = w_all.at[(y, other_y)[n], s, far_q]
        arrived(got, x_recv.at[s, n])
        send(got, got, c_send.at[s, n, 1], c_recv.at[s, n, 1], (core_q, v, y))

    from_virt(first)

    driving_load.wait()
    for i in range(pairs_out):
        for h in range(rows_local // tile):
            flipped = driving_in[i, h * tile:(h + 1) * tile].astype(jnp.float32).T.astype(jnp.bfloat16)
            for j in range(NV):
                driving_tx[j, i, :, h * tile:(h + 1) * tile] = flipped[j * chunk:(j + 1) * chunk]
    for to in (third, second, first):
        send(driving_tx.at[to], driving_rx.at[v], d_send.at[to], d_recv.at[v], (q, to, y))
    own_driving = pltpu.make_async_copy(driving_tx.at[v], driving_rx.at[v], local_sem.at[1])
    own_driving.start()

    from_split(v)
    from_far(v, 1)
    from_virt(second)
    from_split(first)
    from_far(first, 0)
    from_far(first, 1)
    from_virt(third)
    from_split(second)
    from_far(second, 0)
    from_far(second, 1)
    from_split(third)
    from_far(third, 0)
    from_far(third, 1)

    pl.when(owner_y == y)(own_amps.wait)
    for src_half in range(2):
        for src_y in range(NK):
            mine = jnp.logical_and(v == y * 2 + src_half, y == src_y)

            @pl.when(jnp.logical_not(mine))
            def _():
                arrived(amps_rx.at[src_y, src_half], a_recv.at[src_half * NK + src_y])

    rows = pairs_out * chunk
    left = [amps_rx[k].reshape(rows, amps_rx.shape[-1]) for k in range(NK)]
    for s in (v, first, second, third):
        for n in range(NK):
            if n or s is not v:
                split = (y, other_y)[n]
                arrived(w_all.at[split, s, core_q], c_recv.at[s, n, 0])
                arrived(w_all.at[split, s, far_core_q], c_recv.at[s, n, 1])
        ladder = jnp.zeros((rows, rows_local), jnp.float32)
        for k in range(NK):
            block = w_all[k, s].reshape(rows_local, w_all.shape[-1])
            ladder = ladder + lax.dot_general(
                left[k], block, (((1,), (1,)), ((), ())), preferred_element_type=jnp.float32
            )
        ladder_ref[s] = ladder

    for load in other_loads:
        load.wait()
    lane = lax.broadcasted_iota(jnp.int32, (chunk, tile), 1)
    row = lax.broadcasted_iota(jnp.int32, (chunk, tile), 0)
    picked = lane == row + v * chunk
    shifts = []
    for i in range(pairs_out):
        line = energy_ref[pair_tile_ref[i]]
        column = jnp.sum(jnp.where(picked, line, 0.0), axis=1, keepdims=True)
        shifts.append((column, pair_energy_ref[i]))
    per_tile = rows_local // tile
    own_driving.wait()
    for s in (first, second, third):
        arrived(driving_rx.at[s], d_recv.at[s])
    for s in range(NV):
        for i in range(pairs_out):
            column, pair = shifts[i]
            for h in range(per_tile):
                lanes = slice(h * tile, (h + 1) * tile)
                denominator = energy_ref[s * per_tile + h] + column - pair
                value = driving_rx[s, i, :, lanes].astype(jnp.float32)
                value = value + ladder_ref[s, i * chunk:(i + 1) * chunk, lanes]
                out_ref[i, :, s * rows_local + h * tile:s * rows_local + (h + 1) * tile] = (
                    value / denominator
                ).astype(jnp.bfloat16)

    for copy, when in sent:
        if when is None:
            copy.wait_send()
        else:
            pl.when(when)(copy.wait_send)


def fused_body(
    weights, amplitudes, slot_tiles, slot_counts, driving, virt_energy, pair_energy, pair_tile
):
    pairs_in, _, slots, tile, _ = amplitudes.shape
    rows_local, columns = weights.shape
    pairs_out = driving.shape[0]
    chunk = tile // NV
    whole_rows = virt_energy.shape[0]
    bf16 = jnp.bfloat16
    dma = pltpu.SemaphoreType.DMA
    hbm = pl.BlockSpec(memory_space=pltpu.HBM)
    return pl.pallas_call(
        kernel,
        out_shape=jax.ShapeDtypeStruct((pairs_out, chunk, whole_rows), bf16),
        in_specs=[hbm] * 8,
        out_specs=pl.BlockSpec(memory_space=pltpu.VMEM),
        scratch_shapes=[
            pltpu.SMEM((pairs_in, 1, slots), jnp.int32),
            pltpu.SMEM((pairs_in,), jnp.int32),
            pltpu.SMEM((pairs_out,), jnp.int32),
            pltpu.SMEM((pairs_out,), jnp.float32),
            pltpu.VMEM((whole_rows // tile, 1, tile), jnp.float32),
            pltpu.VMEM((NK, NV, NQ, rows_local // NQ, columns), bf16),
            pltpu.VMEM((pairs_in, slots, tile, tile), bf16),
            pltpu.VMEM((pairs_out, rows_local, tile), bf16),
            pltpu.VMEM((NV, pairs_in, chunk, columns), bf16),
            pltpu.VMEM((NK, 2, pairs_in, chunk, columns), bf16),
            pltpu.VMEM((NV, pairs_out, chunk, rows_local), bf16),
            pltpu.VMEM((NV, pairs_out, chunk, rows_local), bf16),
            pltpu.VMEM((NV, pairs_out * chunk, rows_local), jnp.float32),
            dma((8,)),
            dma((NV,)),
            dma((NV,)),
            dma((NV,)),
            dma((NV,)),
            dma((NV, 2)),
            dma((NV, 2)),
            dma((NV, 2, 2)),
            dma((NV, 2, 2)),
            dma((NV,)),
            dma((2 * NK,)),
            dma((NV,)),
            dma((NV,)),
        ],
        compiler_params=pltpu.CompilerParams(
            collective_id=0, has_side_effects=True, vmem_limit_bytes=56 * 1024 * 1024
        ),
        cost_estimate=pl.CostEstimate(
            flops=2 * pairs_out * chunk * whole_rows * columns * NK,
            bytes_accessed=4 * 2 * rows_local * columns,
            transcendentals=0,
        ),
    )(
        slot_tiles,
        slot_counts.reshape(pairs_in),
        pair_tile,
        pair_energy,
        weights.reshape(NQ, rows_local // NQ, columns),
        amplitudes.reshape(pairs_in, slots, tile, tile),
        driving,
        virt_energy.reshape(whole_rows // tile, 1, tile),
    )


def solution(mesh):
    placed = (
        P("virt", "ksplit"),
        P(("pair", "virt"), "ksplit", None, None, None),
        P(("pair", "virt"), "ksplit", None),
        P(("pair", "virt"), "ksplit"),
        P(("pair", "ksplit"), "virt", None),
        P(),
        P(("pair", "ksplit")),
        P(("pair", "ksplit")),
    )
    sizes = dict(mesh.shape)
    plan = (sizes["pair"], sizes["virt"], sizes["ksplit"]) == (NQ, NV, NK)

    def chosen(weights, amplitudes, *rest):
        slots, tile = amplitudes.shape[2], amplitudes.shape[3]
        small = weights.size <= 2 ** 21 and weights.shape[1] == 2 * NK * 2 * tile
        pairs = amplitudes.shape[0] == 2 * NQ * NV
        return jax.shard_map(
            fused_body if plan and small and pairs else gather_body,
            mesh=mesh,
            in_specs=placed,
            out_specs=P(("pair", "ksplit"), "virt", None),
            check_vma=False,
        )(weights, amplitudes, *rest)

    return chosen
```

```python
import jax
import jax.numpy as jnp
from jax import lax
from jax.experimental import pallas as pl
from jax.experimental.pallas import tpu as pltpu
from jax.sharding import PartitionSpec as P

MESH = pl.DeviceIdType.MESH


def gather_body(
    weights, amplitudes, slot_tiles, slot_counts, driving, virt_energy, pair_energy, pair_tile
):
    tile_width = amplitudes.shape[-1]
    slot_number = amplitudes.shape[2]
    rows_local = weights.shape[0]
    blocks_local = weights.shape[1] // tile_width
    split_index = lax.axis_index("ksplit")
    virt_index = lax.axis_index("virt")
    column_tiles = weights.reshape(rows_local, blocks_local, tile_width)
    amps = lax.all_gather(amplitudes, "virt", axis=0, tiled=True)
    tiles = lax.all_gather(slot_tiles, "virt", axis=0, tiled=True)
    counts = lax.all_gather(slot_counts, "virt", axis=0, tiled=True)
    local_ids = tiles[:, 0, :] - split_index * blocks_local
    chosen = jnp.take(column_tiles, local_ids, axis=1)
    live_slot = jnp.arange(slot_number, dtype=jnp.int32)[None, :] < counts
    masked = jnp.where(live_slot[:, :, None, None], amps[:, 0], jnp.zeros((), jnp.bfloat16))
    partial_value = jnp.einsum("apsc,pscb->pab", chosen, masked, preferred_element_type=jnp.float32)
    tile_count = virt_energy.shape[0] // tile_width
    energy_table = virt_energy.reshape(tile_count, tile_width)
    one_hot = (pair_tile[:, None] == jnp.arange(tile_count, dtype=jnp.int32)[None, :]).astype(
        jnp.float32
    )
    cols_energy = jnp.dot(
        one_hot, energy_table, precision=lax.Precision.HIGHEST, preferred_element_type=jnp.float32
    )
    ladder = lax.psum_scatter(
        partial_value.astype(jnp.bfloat16), "ksplit", scatter_dimension=0, tiled=True
    ).astype(jnp.float32)
    rows_energy = lax.dynamic_slice_in_dim(virt_energy, virt_index * rows_local, rows_local)
    denominator = rows_energy[None, :, None] + cols_energy[:, None, :] - pair_energy[:, None, None]
    updated = ((driving.astype(jnp.float32) + ladder) / denominator).astype(jnp.bfloat16)
    flipped = jnp.swapaxes(updated, 1, 2)
    return lax.all_to_all(flipped, "virt", split_axis=1, concat_axis=2, tiled=True)


NQ, NV, NK = 4, 4, 2


def kernel(
    tiles_hbm,
    counts_hbm,
    pair_tile_hbm,
    pair_energy_hbm,
    w_hbm,
    amps_hbm,
    driving_hbm,
    energy_hbm,
    out_hbm,
    tiles_ref,
    counts_ref,
    pair_tile_ref,
    pair_energy_ref,
    energy_ref,
    w_all,
    amps_in,
    driving_in,
    amps_tx,
    amps_rx,
    driving_tx,
    driving_rx,
    ladder_ref,
    out_ref,
    local_sem,
    z_send,
    z_recv,
    y_send,
    y_recv,
    x_send,
    x_recv,
    c_send,
    c_recv,
    a_send,
    a_recv,
    d_send,
    d_recv,
):
    q = lax.axis_index("pair")
    v = lax.axis_index("virt")
    y = lax.axis_index("ksplit")
    other_y = 1 - y
    core_q = q + 1 - 2 * lax.rem(q, 2)
    far_q = lax.rem(q + 2, NQ)
    far_core_q = lax.rem(core_q + 2, NQ)
    first = v + 1 - 2 * lax.rem(v, 2)
    second = 2 - v // 2
    third = 3 - 3 * (v // 2)
    pairs_in, slots, tile, _ = amps_in.shape
    pairs_out = driving_in.shape[0]
    chunk = tile // NV
    block_tiles = amps_tx.shape[-1] // tile
    rows_local = driving_in.shape[1]

    loads = [
        pltpu.make_async_copy(src, dst, local_sem.at[n])
        for n, (src, dst) in enumerate((
            (amps_hbm, amps_in),
            (w_hbm, w_all.at[y, v]),
            (tiles_hbm, tiles_ref),
            (counts_hbm, counts_ref),
            (driving_hbm, driving_in),
            (pair_tile_hbm, pair_tile_ref),
            (pair_energy_hbm, pair_energy_ref),
            (energy_hbm, energy_ref),
        ))
    ]
    for load in loads:
        load.start()
    amps_load, w_load, tiles_load, counts_load, driving_load, *other_loads = loads

    barrier = pltpu.get_barrier_semaphore()
    peers = [(q, lax.rem(v + r, NV), y) for r in range(1, NV)]
    peers += [(q, lax.rem(v + r, NV), other_y) for r in range(NV)]
    peers += [(core_q, v, y), (far_q, v, y), (far_q, v, other_y)]
    for peer in peers:
        pl.semaphore_signal(barrier, inc=1, device_id=peer, device_id_type=MESH)
    w_load.wait()
    pl.semaphore_wait(barrier, len(peers))

    sent = []

    def send(src, dst, send_sem, recv_sem, device, when=None):
        copy = pltpu.make_async_remote_copy(
            src_ref=src, dst_ref=dst, send_sem=send_sem, recv_sem=recv_sem,
            device_id=device, device_id_type=MESH,
        )
        if when is None:
            copy.start()
        else:
            pl.when(when)(copy.start)
        sent.append((copy, when))

    def arrived(dst, sem):
        pltpu.make_async_remote_copy(
            src_ref=dst, dst_ref=dst, send_sem=sem, recv_sem=sem,
            device_id=(core_q, v, y), device_id_type=MESH,
        ).wait_recv()

    own = w_all.at[y, v, q]
    for to in (first, second, third):
        send(own, own, z_send.at[to], z_recv.at[v], (q, to, y))
    send(own, own, y_send.at[v], y_recv.at[v], (q, v, other_y))
    send(own, own, x_send.at[v, 1], x_recv.at[v, 1], (far_q, v, other_y))

    amps_load.wait()
    tiles_load.wait()
    counts_load.wait()
    for i in range(pairs_in):
        count = counts_ref[i]
        loaded = [amps_in[i, s].astype(jnp.float32) for s in range(slots)]
        for t in range(block_tiles):
            total = jnp.zeros((tile, tile), jnp.float32)
            for s in range(slots):
                use = jnp.logical_and(count > s, tiles_ref[i, 0, s] == y * block_tiles + t)
                total = total + jnp.where(use, 1.0, 0.0).astype(jnp.float32) * loaded[s]
            flipped = total.T.astype(jnp.bfloat16)
            for j in range(NV):
                amps_tx[j, i, :, t * tile:(t + 1) * tile] = flipped[j * chunk:(j + 1) * chunk]
    owner_y = v // 2
    half = lax.rem(v, 2)
    a_slot = half * NK + y
    a_dst = amps_rx.at[y, half]
    for to in (third, second, first):
        send(amps_tx.at[to], a_dst, a_send.at[to], a_recv.at[a_slot], (q, to, owner_y))
    own_amps = pltpu.make_async_copy(amps_tx.at[v], a_dst, local_sem.at[0])
    pl.when(owner_y == y)(own_amps.start)
    send(amps_tx.at[v], a_dst, a_send.at[v], a_recv.at[a_slot], (q, v, other_y), owner_y != y)

    def from_virt(s):
        got = w_all.at[y, s, q]
        arrived(got, z_recv.at[s])
        send(got, got, x_send.at[s, 0], x_recv.at[s, 0], (far_q, v, y))
        send(got, got, x_send.at[s, 1], x_recv.at[s, 1], (far_q, v, other_y))
        send(got, got, y_send.at[s], y_recv.at[s], (q, v, other_y))
        send(got, got, c_send.at[s, 0, 0], c_recv.at[s, 0, 0], (core_q, v, y))

    def from_split(s):
        got = w_all.at[other_y, s, q]
        arrived(got, y_recv.at[s])
        send(got, got, c_send.at[s, 1, 0], c_recv.at[s, 1, 0], (core_q, v, y))

    def from_far(s, n):
        got = w_all.at[(y, other_y)[n], s, far_q]
        arrived(got, x_recv.at[s, n])
        send(got, got, c_send.at[s, n, 1], c_recv.at[s, n, 1], (core_q, v, y))

    from_virt(first)
    from_virt(second)
    from_virt(third)

    driving_load.wait()
    for i in range(pairs_out):
        for h in range(rows_local // tile):
            flipped = driving_in[i, h * tile:(h + 1) * tile].astype(jnp.float32).T.astype(jnp.bfloat16)
            for j in range(NV):
                driving_tx[j, i, :, h * tile:(h + 1) * tile] = flipped[j * chunk:(j + 1) * chunk]
    for to in (third, second, first):
        send(driving_tx.at[to], driving_rx.at[v], d_send.at[to], d_recv.at[v], (q, to, y))
    own_driving = pltpu.make_async_copy(driving_tx.at[v], driving_rx.at[v], local_sem.at[1])
    own_driving.start()

    from_split(v)
    from_far(v, 1)
    from_split(first)
    from_far(first, 0)
    from_far(first, 1)
    from_split(second)
    from_far(second, 0)
    from_far(second, 1)
    from_split(third)
    from_far(third, 0)
    from_far(third, 1)

    pl.when(owner_y == y)(own_amps.wait)
    for src_half in range(2):
        for src_y in range(NK):
            mine = jnp.logical_and(v == y * 2 + src_half, y == src_y)

            @pl.when(jnp.logical_not(mine))
            def _():
                arrived(amps_rx.at[src_y, src_half], a_recv.at[src_half * NK + src_y])

    rows = pairs_out * chunk
    left = [amps_rx[k].reshape(rows, amps_rx.shape[-1]) for k in range(NK)]
    for s in (v, first, second, third):
        for n in range(NK):
            if n or s is not v:
                split = (y, other_y)[n]
                arrived(w_all.at[split, s, core_q], c_recv.at[s, n, 0])
                arrived(w_all.at[split, s, far_core_q], c_recv.at[s, n, 1])
        ladder = jnp.zeros((rows, rows_local), jnp.float32)
        for k in range(NK):
            block = w_all[k, s].reshape(rows_local, w_all.shape[-1])
            ladder = ladder + lax.dot_general(
                left[k], block, (((1,), (1,)), ((), ())), preferred_element_type=jnp.float32
            )
        ladder_ref[s] = ladder

    for load in other_loads:
        load.wait()
    lane = lax.broadcasted_iota(jnp.int32, (chunk, tile), 1)
    row = lax.broadcasted_iota(jnp.int32, (chunk, tile), 0)
    picked = lane == row + v * chunk
    shifts = []
    for i in range(pairs_out):
        line = energy_ref[pair_tile_ref[i]]
        column = jnp.sum(jnp.where(picked, line, 0.0), axis=1, keepdims=True)
        shifts.append((column, pair_energy_ref[i]))
    per_tile = rows_local // tile
    own_driving.wait()
    for s in (first, second, third):
        arrived(driving_rx.at[s], d_recv.at[s])
    stores = []
    for i in range(pairs_out):
        for s in range(NV):
            column, pair = shifts[i]
            for h in range(per_tile):
                lanes = slice(h * tile, (h + 1) * tile)
                denominator = energy_ref[s * per_tile + h] + column - pair
                value = driving_rx[s, i, :, lanes].astype(jnp.float32)
                value = value + ladder_ref[s, i * chunk:(i + 1) * chunk, lanes]
                out_ref[i, :, s * rows_local + h * tile:s * rows_local + (h + 1) * tile] = (
                    value / denominator
                ).astype(jnp.bfloat16)
        stores.append(pltpu.make_async_copy(out_ref.at[i], out_hbm.at[i], local_sem.at[2 + i]))
        stores[-1].start()

    for store in stores:
        store.wait()
    for copy, when in sent:
        if when is None:
            copy.wait_send()
        else:
            pl.when(when)(copy.wait_send)


def fused_body(
    weights, amplitudes, slot_tiles, slot_counts, driving, virt_energy, pair_energy, pair_tile
):
    pairs_in, _, slots, tile, _ = amplitudes.shape
    rows_local, columns = weights.shape
    pairs_out = driving.shape[0]
    chunk = tile // NV
    whole_rows = virt_energy.shape[0]
    bf16 = jnp.bfloat16
    dma = pltpu.SemaphoreType.DMA
    hbm = pl.BlockSpec(memory_space=pltpu.HBM)
    return pl.pallas_call(
        kernel,
        out_shape=jax.ShapeDtypeStruct((pairs_out, chunk, whole_rows), bf16),
        in_specs=[hbm] * 8,
        out_specs=hbm,
        scratch_shapes=[
            pltpu.SMEM((pairs_in, 1, slots), jnp.int32),
            pltpu.SMEM((pairs_in,), jnp.int32),
            pltpu.SMEM((pairs_out,), jnp.int32),
            pltpu.SMEM((pairs_out,), jnp.float32),
            pltpu.VMEM((whole_rows // tile, 1, tile), jnp.float32),
            pltpu.VMEM((NK, NV, NQ, rows_local // NQ, columns), bf16),
            pltpu.VMEM((pairs_in, slots, tile, tile), bf16),
            pltpu.VMEM((pairs_out, rows_local, tile), bf16),
            pltpu.VMEM((NV, pairs_in, chunk, columns), bf16),
            pltpu.VMEM((NK, 2, pairs_in, chunk, columns), bf16),
            pltpu.VMEM((NV, pairs_out, chunk, rows_local), bf16),
            pltpu.VMEM((NV, pairs_out, chunk, rows_local), bf16),
            pltpu.VMEM((NV, pairs_out * chunk, rows_local), jnp.float32),
            pltpu.VMEM((pairs_out, chunk, whole_rows), bf16),
            dma((8,)),
            dma((NV,)),
            dma((NV,)),
            dma((NV,)),
            dma((NV,)),
            dma((NV, 2)),
            dma((NV, 2)),
            dma((NV, 2, 2)),
            dma((NV, 2, 2)),
            dma((NV,)),
            dma((2 * NK,)),
            dma((NV,)),
            dma((NV,)),
        ],
        compiler_params=pltpu.CompilerParams(
            collective_id=0, has_side_effects=True, vmem_limit_bytes=56 * 1024 * 1024
        ),
        cost_estimate=pl.CostEstimate(
            flops=2 * pairs_out * chunk * whole_rows * columns * NK,
            bytes_accessed=4 * 2 * rows_local * columns,
            transcendentals=0,
        ),
    )(
        slot_tiles,
        slot_counts.reshape(pairs_in),
        pair_tile,
        pair_energy,
        weights.reshape(NQ, rows_local // NQ, columns),
        amplitudes.reshape(pairs_in, slots, tile, tile),
        driving,
        virt_energy.reshape(whole_rows // tile, 1, tile),
    )


def solution(mesh):
    placed = (
        P("virt", "ksplit"),
        P(("pair", "virt"), "ksplit", None, None, None),
        P(("pair", "virt"), "ksplit", None),
        P(("pair", "virt"), "ksplit"),
        P(("pair", "ksplit"), "virt", None),
        P(),
        P(("pair", "ksplit")),
        P(("pair", "ksplit")),
    )
    sizes = dict(mesh.shape)
    plan = (sizes["pair"], sizes["virt"], sizes["ksplit"]) == (NQ, NV, NK)

    def chosen(weights, amplitudes, *rest):
        slots, tile = amplitudes.shape[2], amplitudes.shape[3]
        small = weights.size <= 2 ** 21 and weights.shape[1] == 2 * NK * 2 * tile
        pairs = amplitudes.shape[0] == 2 * NQ * NV
        return jax.shard_map(
            fused_body if plan and small and pairs else gather_body,
            mesh=mesh,
            in_specs=placed,
            out_specs=P(("pair", "ksplit"), "virt", None),
            check_vma=False,
        )(weights, amplitudes, *rest)

    return chosen
```
